512 devices in a mesh: dp: 16 (over x, z_hi), ctx: 32 (over y, z_lo, core).
Axes of the slice: x: 4, y: 8, z: 8 (z_hi: 4, z_lo: 2; z = z_hi * 2 + z_lo), core: 2. Of those that a mesh axis runs over, the one named last changes fastest.
Arguments:
- u_saved: bfloat16 [16, 4096, 2048], P('dp', 'ctx'), may hold values from -6 to 6
- grad_out: bfloat16 [16, 4096, 2048], P('dp', 'ctx'), may hold values from -6 to 6
- filters: bfloat16 [4096, 128], P('ctx'), may hold values from -2 to 2
Outputs:
- input_grad: bfloat16 [16, 4096, 2048], P('dp', 'ctx')
- filter_grad: float32 [4096, 128], P('ctx', 'dp')
The draws below stay inside these ranges and needn't reach their ends.
All inputs are finite; a program needn't handle non-finite values.
Results may differ from the reference program's by a relative error of at most 0.001.
Values may be sent and summed in bfloat16 or wider, within the bound.
No kernel may reach another device: no remote copies, remote signals or barrier semaphores. Data moves between devices by JAX's collectives and lax.ppermute only.
A program may use at most 128 MiB of HBM per device.

```python
import math
import jax
import jax.numpy as jnp
from jax import lax

CH = 2048
GROUP = 16
GROUPS = 128
LENGTH = 4096
SEQS = 16


def draw_filters(key, part):
    subkeys = jax.random.split(key, 4)
    lag_index = jnp.arange(LENGTH, dtype=jnp.float32)[:, None]
    slow_share = 0.5
    slow_group = jax.random.bernoulli(subkeys[0], slow_share, (GROUPS,))
    slow_scale = LENGTH * jnp.exp(jax.random.uniform(subkeys[1], (GROUPS,), jnp.float32, math.log(0.5), math.log(4.0)))
    fast_scale = jnp.exp(jax.random.uniform(subkeys[2], (GROUPS,), jnp.float32, math.log(8.0), math.log(40.0)))
    time_scale = jnp.where(slow_group, slow_scale, fast_scale)
    random_part = jax.random.truncated_normal(subkeys[3], -4.0, 4.0, (LENGTH, GROUPS), jnp.float32)
    return (random_part * jnp.exp(-lag_index / time_scale) * jnp.sqrt(2.0 / time_scale)).astype(jnp.bfloat16)


def spiked(array, stream_key, source, target, shards_of, factor):
    def block_of(dim):
        return (jnp.arange(array.shape[dim]) // (array.shape[dim] // shards_of)).reshape((-1,) + (1,) * (array.ndim - 1 - dim))

    first = jax.random.permutation(stream_key, shards_of)[block_of(target)]
    other_side = (block_of(target) + shards_of // 2) % shards_of
    return jnp.where((block_of(source) == first) | (block_of(source) == other_side), factor * array, array)


def level_of(stream_key, shape, cuts, smallest, high):
    gain, own = 1.0, jax.random.fold_in(stream_key, 6)
    for position, parts in cuts:
        heights = jnp.exp(jax.random.uniform(jax.random.fold_in(own, position), (parts,), jnp.float32, smallest / len(cuts), high / len(cuts)))
        gain = gain * jnp.repeat(heights, shape[position] // parts).reshape([-1 if axis == position else 1 for axis in range(len(shape))])
    return gain


def noise(key, dims, spread, most, pieces=(), kind=jnp.bfloat16):
    drawn = jax.random.normal(key, dims, jnp.float32) * spread
    if len(pieces) > 0:
        drawn = level_of(key, dims, pieces, -0.22, 0.18) * drawn
    return jnp.clip(drawn, min=-most, max=most).astype(kind)


def bell_draw_with(rng, dims, scale, bound, pieces, heavy, held_as=jnp.bfloat16):
    result = scale * jax.random.normal(rng, dims, jnp.float32)
    if pieces:
        result = result * level_of(rng, dims, pieces, -0.22, 0.18)
    return jnp.clip(spiked(result, jax.random.fold_in(rng, 3), *heavy), -bound, bound).astype(held_as)


def setup_inputs(seed: int = 0) -> dict:
    streams_of = jax.random.split(jax.random.key(seed), 4)
    u_saved = noise(streams_of[0], (SEQS, LENGTH, CH), 1.0, 6.0, ((0, 16), (1, 32)))
    grad_out = bell_draw_with(streams_of[1], (SEQS, LENGTH, CH), 1.0, 6.0, ((0, 16), (1, 32)), (0, 2, 16, 2.0))
    filters = draw_filters(jax.random.fold_in(streams_of[3], 71), 0)
    return dict(u_saved=u_saved, grad_out=grad_out, filters=filters)


def reference(u_saved, grad_out, filters):
    padded = 2 * LENGTH
    kernel_spec = jnp.fft.fft(filters.astype(jnp.float32), n=padded, axis=0)
    kernel_wide = jnp.repeat(kernel_spec, GROUP, axis=1)

    def sequence_step(carry, pair):
        saved_seq, grad_seq = pair
        saved_spec = jnp.fft.fft(saved_seq.astype(jnp.float32), n=padded, axis=0)
        grad_spec = jnp.fft.fft(grad_seq.astype(jnp.float32), n=padded, axis=0)
        input_part = jnp.real(jnp.fft.ifft(jnp.conj(kernel_wide) * grad_spec, axis=0))[:LENGTH]
        product = (grad_spec * jnp.conj(saved_spec)).reshape(padded, GROUPS, GROUP).sum(axis=2)
        new_carry = (carry[0] + jnp.real(product), carry[1] + jnp.imag(product))
        return (new_carry, input_part.astype(jnp.bfloat16))
    zero_sum = jnp.zeros((padded, GROUPS), jnp.float32)
    sums, input_grad = lax.scan(sequence_step, (zero_sum, zero_sum), (u_saved, grad_out))
    group_spec = lax.complex(sums[0], sums[1])
    filter_grad = jnp.real(jnp.fft.ifft(group_spec, axis=0))[:LENGTH]
    filter_grad = filter_grad / jnp.sqrt(jnp.float32(GROUP * SEQS * LENGTH))
    return (input_grad, filter_grad.astype(jnp.float32))
```

```python
import functools

import jax
import jax.numpy as jnp
from jax import lax
from jax.experimental import pallas as pl
from jax.experimental.pallas import tpu as pltpu
from jax.sharding import PartitionSpec as P

GROUP = 16
LANES = 128
VMEM_LIMIT = 56 * 1024 * 1024


def widen_blocks(blocks_ref, group, wide_ref):
    parts = blocks_ref.shape[0]
    first = pl.multiple_of(group * GROUP, GROUP)
    for part in range(parts):
        row = (part // 2) * GROUP
        lane = (part % 2) * LANES
        wide_ref[row : row + GROUP, lane : lane + LANES] = blocks_ref[
            part, pl.ds(first, GROUP), :
        ]


def input_kernel(grad_ref, filt_ref, out_ref, wide_ref, toep_ref):
    parts, channels, _ = grad_ref.shape
    half = parts // 2
    rows = half * GROUP
    span = 2 * LANES
    wide_ref[rows:, :] = jnp.zeros_like(wide_ref[rows:, :])

    def per_group(group, carry):
        widen_blocks(grad_ref, group, wide_ref)
        line = filt_ref[pl.ds(group, 1), :]
        spread = jnp.broadcast_to(line, (LANES, line.shape[1]))
        toep_ref[...] = pltpu.roll(spread, 0, 1, stride=1, stride_axis=0).astype(jnp.bfloat16)
        total = jnp.zeros((rows, span), jnp.float32)
        for lag in range(half):
            start = lag * span
            taps = jnp.concatenate(
                [
                    toep_ref[:, start + LANES : start + LANES + span],
                    toep_ref[:, start : start + span],
                ],
                axis=0,
            )
            total = total + lax.dot_general(
                wide_ref[lag * GROUP : lag * GROUP + rows, :],
                taps,
                (((1,), (1,)), ((), ())),
                preferred_element_type=jnp.float32,
            )
        done = total.astype(jnp.bfloat16)
        first = pl.multiple_of(group * GROUP, GROUP)
        for part in range(parts):
            row = (part // 2) * GROUP
            lane = (part % 2) * LANES
            out_ref[part, pl.ds(first, GROUP), :] = done[
                row : row + GROUP, lane : lane + LANES
            ]
        return carry

    lax.fori_loop(0, channels // GROUP, per_group, 0)


def filter_kernel(grad_ref, saved_ref, out_ref, wide_ref, saved_wide_ref, toep_ref):
    parts, channels, _ = grad_ref.shape
    half = parts // 2
    rows = half * GROUP
    span = 2 * LANES
    length = parts * LANES
    wide_ref[rows:, :] = jnp.zeros_like(wide_ref[rows:, :])
    row_ids = lax.broadcasted_iota(jnp.int32, (span, span), 0)
    col_ids = lax.broadcasted_iota(jnp.int32, (span, span), 1)
    mirror = (row_ids // LANES) * LANES + (LANES - 1 - row_ids % LANES)
    flip = jnp.where(mirror == col_ids, 1.0, 0.0).astype(jnp.bfloat16)

    def per_group(group, carry):
        widen_blocks(grad_ref, group, wide_ref)
        widen_blocks(saved_ref, group, saved_wide_ref)
        saved_lag = lax.dot_general(
            flip,
            saved_wide_ref[...],
            (((1,), (1,)), ((), ())),
            preferred_element_type=jnp.float32,
        ).astype(jnp.bfloat16)
        toep_ref[...] = jnp.zeros_like(toep_ref)
        for lag in range(half):
            start = lag * span
            piece = jnp.dot(
                saved_lag,
                wide_ref[lag * GROUP : lag * GROUP + rows, :],
                preferred_element_type=jnp.float32,
            )
            toep_ref[:, start + LANES : start + LANES + span] += piece[:LANES, :]
            toep_ref[:, start : start + span] += piece[LANES:, :]
        turned = pltpu.roll(toep_ref[...], 1, 1, stride=1, stride_axis=0)
        out_ref[pl.ds(group, 1), :] = jnp.sum(turned, axis=0, keepdims=True)[
            :, span : span + length
        ]
        return carry

    lax.fori_loop(0, channels // GROUP, per_group, 0)


def input_pass(grad_blocks, filter_line):
    parts, channels, _ = grad_blocks.shape
    rows = parts // 2 * GROUP
    return pl.pallas_call(
        input_kernel,
        out_shape=jax.ShapeDtypeStruct(grad_blocks.shape, jnp.bfloat16),
        scratch_shapes=[
            pltpu.VMEM((2 * rows, 2 * LANES), jnp.bfloat16),
            pltpu.VMEM((LANES, filter_line.shape[1]), jnp.bfloat16),
        ],
        compiler_params=pltpu.CompilerParams(vmem_limit_bytes=VMEM_LIMIT),
        cost_estimate=pl.CostEstimate(flops=2**31, bytes_accessed=2**20, transcendentals=0),
    )(grad_blocks, filter_line)


def filter_pass(grad_blocks, saved_blocks):
    parts, channels, _ = grad_blocks.shape
    rows = parts // 2 * GROUP
    length = parts * LANES
    return pl.pallas_call(
        filter_kernel,
        out_shape=jax.ShapeDtypeStruct((channels // GROUP, length), jnp.float32),
        scratch_shapes=[
            pltpu.VMEM((2 * rows, 2 * LANES), jnp.bfloat16),
            pltpu.VMEM((rows, 2 * LANES), jnp.bfloat16),
            pltpu.VMEM((LANES, length + 2 * LANES), jnp.float32),
        ],
        compiler_params=pltpu.CompilerParams(vmem_limit_bytes=VMEM_LIMIT),
        cost_estimate=pl.CostEstimate(flops=2**31, bytes_accessed=2**20, transcendentals=0),
    )(grad_blocks, saved_blocks)


def to_channels(tokens_by_channel, parts):
    turned = tokens_by_channel.T
    blocks = turned.reshape(parts, turned.shape[0] // parts, turned.shape[1])
    return lax.all_to_all(blocks, "ctx", split_axis=0, concat_axis=0, tiled=True)


def on_device(u_saved, grad_out, filters):
    parts = lax.axis_size("ctx")
    seqs = lax.axis_size("dp")
    filter_blocks = to_channels(filters, parts)
    grad_blocks = to_channels(grad_out[0], parts)
    saved_blocks = to_channels(u_saved[0], parts)
    groups_here = filter_blocks.shape[1]
    length = parts * filter_blocks.shape[2]
    line = filter_blocks.transpose(1, 0, 2).reshape(groups_here, length).astype(jnp.float32)
    line = jnp.pad(line, ((0, 0), (LANES, LANES)))
    input_blocks = input_pass(grad_blocks, line)
    returned = lax.all_to_all(input_blocks, "ctx", split_axis=0, concat_axis=0, tiled=True)
    input_grad = returned.reshape(-1, returned.shape[2]).T[None]
    group_lags = filter_pass(grad_blocks, saved_blocks)
    lag_blocks = group_lags.reshape(groups_here, parts, -1).transpose(1, 0, 2)
    lag_moved = lax.all_to_all(lag_blocks, "ctx", split_axis=0, concat_axis=0, tiled=True)
    by_group = lag_moved.reshape(-1, lag_moved.shape[2])
    filter_part = lax.psum_scatter(by_group, "dp", scatter_dimension=0, tiled=True)
    filter_grad = filter_part.T / jnp.sqrt(jnp.float32(GROUP * seqs * length))
    return (input_grad, filter_grad)


def solution(mesh):
    in_specs = (P("dp", "ctx", None), P("dp", "ctx", None), P("ctx", None))
    out_specs = (P("dp", "ctx", None), P("ctx", "dp"))
    return jax.shard_map(
        on_device, mesh=mesh, in_specs=in_specs, out_specs=out_specs, check_vma=False
    )
```

```python
import math

import jax
import jax.numpy as jnp
from jax import lax
from jax.experimental import pallas as pl
from jax.experimental.pallas import tpu as pltpu
from jax.sharding import PartitionSpec as P

GROUP = 16
LANES = 128
SPAN = 2 * LANES
SIDE = 4
MIB = 1024 * 1024


def call(kernel, out_shape, *operands, scratch=(), flops=2**20, vmem=2 * MIB):
    in_vmem = pl.BlockSpec(memory_space=pltpu.VMEM)
    several = isinstance(out_shape, (list, tuple))
    return pl.pallas_call(
        kernel,
        out_shape=out_shape,
        in_specs=[in_vmem] * len(operands),
        out_specs=[in_vmem] * len(out_shape) if several else in_vmem,
        scratch_shapes=list(scratch),
        compiler_params=pltpu.CompilerParams(vmem_limit_bytes=vmem),
        cost_estimate=pl.CostEstimate(flops=flops, bytes_accessed=2**20, transcendentals=0),
    )(*operands)


def pack_kernel(saved_ref, grad_ref, filt_ref, out_ref):
    parts, rows, _ = out_ref.shape
    channels = saved_ref.shape[1] // parts
    groups = filt_ref.shape[1] // parts
    per_tile = LANES // channels
    for tile in range(parts // per_tile):
        cols = slice(tile * LANES, (tile + 1) * LANES)
        grad_rows = grad_ref[:, cols].T
        saved_rows = saved_ref[:, cols].T
        for inner in range(per_tile):
            part = tile * per_tile + inner
            mine = slice(inner * channels, (inner + 1) * channels)
            out_ref[part, :channels, :] = grad_rows[mine, :]
            out_ref[part, channels : 2 * channels, :] = saved_rows[mine, :]
    lines = filt_ref[...].astype(jnp.float32).T
    tail = rows - 2 * channels
    for part in range(parts):
        mine = lines[part * groups : (part + 1) * groups, :]
        block = jnp.concatenate([mine, jnp.zeros((tail - groups, LANES), jnp.float32)], axis=0)
        out_ref[part, 2 * channels :, :] = block.astype(jnp.bfloat16)


def widen_blocks(blocks_ref, first, wide_ref):
    for part in range(blocks_ref.shape[0]):
        row = (part // 2) * GROUP
        lane = (part % 2) * LANES
        wide_ref[row : row + GROUP, lane : lane + LANES] = blocks_ref[
            part, pl.ds(first, GROUP), :
        ]


def input_kernel(blocks_ref, out_ref, line_ref, wide_ref, toep_ref):
    parts, channels, _ = out_ref.shape
    groups = channels // GROUP
    half = parts // 2
    rows = half * GROUP
    wide_ref[rows:, :] = jnp.zeros_like(wide_ref[rows:, :])
    line_ref[...] = jnp.zeros_like(line_ref)
    for part in range(parts):
        start = (part + 1) * LANES
        line_ref[:, start : start + LANES] = blocks_ref[part, 2 * channels :, :][
            : line_ref.shape[0]
        ].astype(jnp.float32)

    def per_group(group, carry):
        first = pl.multiple_of(group * GROUP, GROUP)
        widen_blocks(blocks_ref, first, wide_ref)
        line = line_ref[pl.ds(group, 1), :]
        spread = jnp.broadcast_to(line, (LANES, line.shape[1]))
        toep_ref[...] = pltpu.roll(spread, 0, 1, stride=1, stride_axis=0).astype(jnp.bfloat16)
        total = jnp.zeros((rows, SPAN), jnp.float32)
        for lag in range(half):
            start = lag * SPAN
            taps = jnp.concatenate(
                [
                    toep_ref[:, start + LANES : start + LANES + SPAN],
                    toep_ref[:, start : start + SPAN],
                ],
                axis=0,
            )
            total = total + lax.dot_general(
                wide_ref[lag * GROUP : lag * GROUP + rows, :],
                taps,
                (((1,), (1,)), ((), ())),
                preferred_element_type=jnp.float32,
            )
        done = total.astype(jnp.bfloat16)
        for part in range(parts):
            row = (part // 2) * GROUP
            lane = (part % 2) * LANES
            out_ref[part, pl.ds(first, GROUP), :] = done[
                row : row + GROUP, lane : lane + LANES
            ]
        return carry

    lax.fori_loop(0, groups, per_group, 0)


def filter_kernel(side_of, blocks_ref, *refs):
    out_refs, (wide_ref, saved_wide_ref, toep_ref, sums_ref) = refs[:SIDE], refs[SIDE:]
    parts, rows_all, _ = blocks_ref.shape
    half = parts // 2
    rows = half * GROUP
    groups = sums_ref.shape[1]
    channels = groups * GROUP
    wide_ref[rows:, :] = jnp.zeros_like(wide_ref[rows:, :])
    row_ids = lax.broadcasted_iota(jnp.int32, (SPAN, SPAN), 0)
    col_ids = lax.broadcasted_iota(jnp.int32, (SPAN, SPAN), 1)
    mirror = (row_ids // LANES) * LANES + (LANES - 1 - row_ids % LANES)
    flip = jnp.where(mirror == col_ids, 1.0, 0.0).astype(jnp.bfloat16)

    def per_group(group, carry):
        first = pl.multiple_of(group * GROUP, GROUP)
        widen_blocks(blocks_ref, first, wide_ref)
        widen_blocks(blocks_ref, first + channels, saved_wide_ref)
        saved_lag = lax.dot_general(
            flip,
            saved_wide_ref[...],
            (((1,), (1,)), ((), ())),
            preferred_element_type=jnp.float32,
        ).astype(jnp.bfloat16)
        toep_ref[...] = jnp.zeros_like(toep_ref)
        for lag in range(half):
            start = lag * SPAN
            piece = jnp.dot(
                saved_lag,
                wide_ref[lag * GROUP : lag * GROUP + rows, :],
                preferred_element_type=jnp.float32,
            )
            toep_ref[:, start + LANES : start + LANES + SPAN] += piece[:LANES, :]
            toep_ref[:, start : start + SPAN] += piece[LANES:, :]
        turned = pltpu.roll(toep_ref[...], 1, 1, stride=1, stride_axis=0)
        line = jnp.sum(turned, axis=0, keepdims=True)
        for part in range(parts):
            start = SPAN + part * LANES
            sums_ref[part, pl.ds(group, 1), :] = line[:, start : start + LANES]
        return carry

    lax.fori_loop(0, groups, per_group, 0)
    share = parts // SIDE
    side = side_of()
    for step in range(SIDE):
        first = lax.rem(side + step, SIDE) * share
        out_refs[step][...] = sums_ref[pl.ds(first, share)]


def join_kernel(side_of, *refs):
    in_refs, out_refs = refs[:SIDE], refs[SIDE:]
    count = len(out_refs)
    total = in_refs[0][...] + in_refs[1][...] + in_refs[2][...] + in_refs[3][...]
    share = total.shape[0] // count
    side = side_of()
    for step in range(count):
        place = lax.rem(side + step, count)
        value = total[:share]
        for other in range(1, count):
            value = jnp.where(place == other, total[other * share : (other + 1) * share], value)
        out_refs[step][...] = value


def last_kernel(side_of, scale, near_ref, far_ref, out_ref):
    near, far = near_ref[0] * scale, far_ref[0] * scale
    even = side_of() == 0
    first = jnp.where(even, near, far)
    second = jnp.where(even, far, near)
    out_ref[...] = jnp.concatenate([first, second], axis=0)


def shifted(step, stride):
    moves = []
    for device in range(SIDE * SIDE):
        place = device // stride % SIDE
        moves.append((device, device + ((place + step) % SIDE - place) * stride))
    return moves


def on_device(u_saved, grad_out, filters):
    parts = lax.axis_size("ctx")
    seqs = lax.axis_size("dp")
    channels = u_saved.shape[2] // parts
    groups = channels // GROUP
    length = parts * LANES
    bf16, f32 = jnp.bfloat16, jnp.float32
    half_rows = parts // 2 * GROUP

    packed = call(
        pack_kernel,
        jax.ShapeDtypeStruct((parts, 2 * channels + 8, LANES), bf16),
        u_saved[0],
        grad_out[0],
        filters,
        vmem=8 * MIB,
    )
    blocks = lax.all_to_all(packed, "ctx", split_axis=0, concat_axis=0, tiled=True)
    input_blocks = call(
        input_kernel,
        jax.ShapeDtypeStruct((parts, channels, LANES), bf16),
        blocks,
        scratch=[
            pltpu.VMEM((groups, length + SPAN), f32),
            pltpu.VMEM((2 * half_rows, SPAN), bf16),
            pltpu.VMEM((LANES, length + SPAN), bf16),
        ],
        flops=2**31,
        vmem=20 * MIB,
    )
    returned = lax.all_to_all(input_blocks, "ctx", split_axis=0, concat_axis=0, tiled=True)

    def slow_side():
        return lax.axis_index("dp") // SIDE

    def fast_side():
        return lax.rem(lax.axis_index("dp"), SIDE)

    def parity():
        return lax.rem(lax.axis_index("ctx"), 2)

    shares = call(
        lambda *refs: filter_kernel(slow_side, *refs),
        [jax.ShapeDtypeStruct((parts // SIDE, groups, LANES), f32)] * SIDE,
        blocks,
        scratch=[
            pltpu.VMEM((2 * half_rows, SPAN), bf16),
            pltpu.VMEM((half_rows, SPAN), bf16),
            pltpu.VMEM((LANES, length + SPAN), f32),
            pltpu.VMEM((parts, groups, LANES), f32),
        ],
        flops=2**31,
        vmem=20 * MIB,
    )
    came = [shares[0]] + [
        lax.ppermute(shares[step], "dp", shifted(step, SIDE)) for step in range(1, SIDE)
    ]
    shares = call(
        lambda *refs: join_kernel(fast_side, *refs),
        [jax.ShapeDtypeStruct((parts // SIDE**2, groups, LANES), f32)] * SIDE,
        *came,
    )
    came = [shares[0]] + [
        lax.ppermute(shares[step], "dp", shifted(step, 1)) for step in range(1, SIDE)
    ]
    near, far = call(
        lambda *refs: join_kernel(parity, *refs),
        [jax.ShapeDtypeStruct((1, groups, LANES), f32)] * 2,
        *came,
    )
    near_moves, far_moves = [], []
    for seq in range(seqs):
        for part in range(parts):
            here = seq * parts + part
            base = (part // 2) * parts + 2 * seq
            near_moves.append((here, base + part % 2))
            far_moves.append((here, base + 1 - part % 2))
    near = lax.ppermute(near, ("dp", "ctx"), near_moves)
    far = lax.ppermute(far, ("dp", "ctx"), far_moves)
    scale = 1.0 / math.sqrt(GROUP * seqs * length)
    filter_part = call(
        lambda *refs: last_kernel(parity, scale, *refs),
        jax.ShapeDtypeStruct((2 * groups, LANES), f32),
        near,
        far,
    )
    input_grad = returned.reshape(-1, LANES).T[None]
    return (input_grad, filter_part.T)


def solution(mesh):
    in_specs = (P("dp", "ctx", None), P("dp", "ctx", None), P("ctx", None))
    out_specs = (P("dp", "ctx", None), P("ctx", "dp"))
    return jax.shard_map(
        on_device, mesh=mesh, in_specs=in_specs, out_specs=out_specs, check_vma=False
    )
```

```python
import math

import jax
import jax.numpy as jnp
from jax import lax
from jax.experimental import pallas as pl
from jax.experimental.pallas import tpu as pltpu
from jax.sharding import Mesh, PartitionSpec as P

GROUP = 16
LANES = 128
SPAN = 2 * LANES
SIDE = 4
MIB = 1024 * 1024
PACK_VMEM = 8 * MIB


def call(kernel, out_shape, *operands, scratch=(), flops=2**20, vmem=2 * MIB):
    in_vmem = pl.BlockSpec(memory_space=pltpu.VMEM)
    several = isinstance(out_shape, (list, tuple))
    return pl.pallas_call(
        kernel,
        out_shape=out_shape,
        in_specs=[in_vmem] * len(operands),
        out_specs=[in_vmem] * len(out_shape) if several else in_vmem,
        scratch_shapes=list(scratch),
        compiler_params=pltpu.CompilerParams(vmem_limit_bytes=vmem),
        cost_estimate=pl.CostEstimate(flops=flops, bytes_accessed=2**20, transcendentals=0),
    )(*operands)


def pack_kernel(saved_ref, grad_ref, filt_ref, out_ref, lines_ref):
    places, groups = LANES // GROUP, SIDE
    channels = groups * GROUP
    for tile in range(groups * SIDE):
        slot, inner = tile // SIDE, tile % SIDE
        cols = slice(tile * LANES, (tile + 1) * LANES)
        grad_rows = grad_ref[:, cols].T
        saved_rows = saved_ref[:, cols].T
        for place in range(places):
            part = place * SIDE + inner
            mine = slice(place * GROUP, (place + 1) * GROUP)
            row = slot * GROUP
            out_ref[part, row : row + GROUP, :] = grad_rows[mine, :]
            out_ref[part, channels + row : channels + row + GROUP, :] = saved_rows[mine, :]
    lines_ref[...] = filt_ref[...].astype(jnp.float32).T
    empty = jnp.zeros((out_ref.shape[1] - 2 * channels - groups, LANES), jnp.float32)
    for place in range(places):
        for inner in range(SIDE):
            first = inner * places + place
            mine = lines_ref[pl.ds(first, groups, stride=SIDE * places), :]
            block = jnp.concatenate([mine, empty], axis=0)
            out_ref[place * SIDE + inner, 2 * channels :, :] = block.astype(jnp.bfloat16)


def unpack_kernel(blocks_ref, out_ref):
    places = LANES // GROUP
    for tile in range(out_ref.shape[1] // LANES):
        slot, inner = tile // SIDE, tile % SIDE
        row = slot * GROUP
        rows = [
            blocks_ref[place * SIDE + inner, row : row + GROUP, :] for place in range(places)
        ]
        out_ref[:, tile * LANES : (tile + 1) * LANES] = jnp.concatenate(rows, axis=0).T


def widen_blocks(blocks_ref, first, wide_ref):
    for part in range(blocks_ref.shape[0]):
        row = (part // 2) * GROUP
        lane = (part % 2) * LANES
        wide_ref[row : row + GROUP, lane : lane + LANES] = blocks_ref[
            part, pl.ds(first, GROUP), :
        ]


def input_kernel(blocks_ref, out_ref, line_ref, wide_ref, toep_ref):
    parts, channels, _ = out_ref.shape
    groups = channels // GROUP
    half = parts // 2
    rows = half * GROUP
    wide_ref[rows:, :] = jnp.zeros_like(wide_ref[rows:, :])
    line_ref[...] = jnp.zeros_like(line_ref)
    for part in range(parts):
        start = (part + 1) * LANES
        line_ref[:, start : start + LANES] = blocks_ref[part, 2 * channels :, :][
            : line_ref.shape[0]
        ].astype(jnp.float32)

    def per_group(group, carry):
        first = pl.multiple_of(group * GROUP, GROUP)
        widen_blocks(blocks_ref, first, wide_ref)
        line = line_ref[pl.ds(group, 1), :]
        spread = jnp.broadcast_to(line, (LANES, line.shape[1]))
        toep_ref[...] = pltpu.roll(spread, 0, 1, stride=1, stride_axis=0).astype(jnp.bfloat16)
        total = jnp.zeros((rows, SPAN), jnp.float32)
        for lag in range(half):
            start = lag * SPAN
            taps = jnp.concatenate(
                [
                    toep_ref[:, start + LANES : start + LANES + SPAN],
                    toep_ref[:, start : start + SPAN],
                ],
                axis=0,
            )
            total = total + lax.dot_general(
                wide_ref[lag * GROUP : lag * GROUP + rows, :],
                taps,
                (((1,), (1,)), ((), ())),
                preferred_element_type=jnp.float32,
            )
        done = total.astype(jnp.bfloat16)
        for part in range(parts):
            row = (part // 2) * GROUP
            lane = (part % 2) * LANES
            out_ref[part, pl.ds(first, GROUP), :] = done[
                row : row + GROUP, lane : lane + LANES
            ]
        return carry

    lax.fori_loop(0, groups, per_group, 0)


def filter_kernel(blocks_ref, out_ref, wide_ref, saved_wide_ref, toep_ref):
    parts, _, _ = blocks_ref.shape
    half = parts // 2
    rows = half * GROUP
    groups = SIDE
    places = parts // SIDE
    channels = groups * GROUP
    wide_ref[rows:, :] = jnp.zeros_like(wide_ref[rows:, :])
    row_ids = lax.broadcasted_iota(jnp.int32, (SPAN, SPAN), 0)
    col_ids = lax.broadcasted_iota(jnp.int32, (SPAN, SPAN), 1)
    mirror = (row_ids // LANES) * LANES + (LANES - 1 - row_ids % LANES)
    flip = jnp.where(mirror == col_ids, 1.0, 0.0).astype(jnp.bfloat16)

    def per_group(group, carry):
        first = pl.multiple_of(group * GROUP, GROUP)
        widen_blocks(blocks_ref, first, wide_ref)
        widen_blocks(blocks_ref, first + channels, saved_wide_ref)
        saved_lag = lax.dot_general(
            flip,
            saved_wide_ref[...],
            (((1,), (1,)), ((), ())),
            preferred_element_type=jnp.float32,
        ).astype(jnp.bfloat16)
        toep_ref[...] = jnp.zeros_like(toep_ref)
        for lag in range(half):
            start = lag * SPAN
            piece = jnp.dot(
                saved_lag,
                wide_ref[lag * GROUP : lag * GROUP + rows, :],
                preferred_element_type=jnp.float32,
            )
            toep_ref[:, start + LANES : start + LANES + SPAN] += piece[:LANES, :]
            toep_ref[:, start : start + SPAN] += piece[LANES:, :]
        turned = pltpu.roll(toep_ref[...], 1, 1, stride=1, stride_axis=0)
        line = jnp.sum(turned, axis=0, keepdims=True)
        for part in range(parts):
            start = SPAN + part * LANES
            inner = part % SIDE
            out_ref[group * places + part // SIDE, inner : inner + 1, :] = line[
                :, start : start + LANES
            ]
        return carry

    lax.fori_loop(0, groups, per_group, 0)


def join_kernel(came_ref, *out_refs):
    places = came_ref.shape[0] // SIDE
    total = came_ref[:places]
    for step in range(1, SIDE):
        total = total + came_ref[step * places : (step + 1) * places]
    side = lax.axis_index("zh")
    for step in range(SIDE):
        inner = lax.rem(side + step, SIDE)
        value = total[:, 0, :]
        for other in range(1, SIDE):
            value = jnp.where(inner == other, total[:, other, :], value)
        out_refs[step][...] = value


def last_kernel(scale, *refs):
    in_refs, out_ref = refs[:SIDE], refs[SIDE]
    total = in_refs[0][...] + in_refs[1][...] + in_refs[2][...] + in_refs[3][...]
    out_ref[...] = total * scale


def on_device(u_saved, grad_out, filters):
    tokens, width = u_saved.shape[1:]
    parts = lax.axis_size(("y", "w"))
    seqs = lax.axis_size(("x", "zh"))
    places = lax.axis_size("y")
    channels = width // parts
    groups = channels // GROUP
    length = parts * LANES
    bf16, f32 = jnp.bfloat16, jnp.float32
    half_rows = parts // 2 * GROUP

    packed = call(
        pack_kernel,
        jax.ShapeDtypeStruct((parts, 2 * channels + 8, LANES), bf16),
        u_saved[0],
        grad_out[0],
        filters,
        scratch=[pltpu.VMEM((LANES, LANES), f32)],
        vmem=PACK_VMEM,
    )
    blocks = lax.all_to_all(packed, ("y", "w"), split_axis=0, concat_axis=0, tiled=True)
    lags = call(
        filter_kernel,
        jax.ShapeDtypeStruct((parts, SIDE, LANES), f32),
        blocks,
        scratch=[
            pltpu.VMEM((2 * half_rows, SPAN), bf16),
            pltpu.VMEM((half_rows, SPAN), bf16),
            pltpu.VMEM((LANES, length + SPAN), f32),
        ],
        flops=2**31,
        vmem=20 * MIB,
    )
    lags_came = lax.all_to_all(lags, ("x", "y"), split_axis=0, concat_axis=0, tiled=True)
    input_blocks = call(
        input_kernel,
        jax.ShapeDtypeStruct((parts, channels, LANES), bf16),
        blocks,
        scratch=[
            pltpu.VMEM((groups, length + SPAN), f32),
            pltpu.VMEM((2 * half_rows, SPAN), bf16),
            pltpu.VMEM((LANES, length + SPAN), bf16),
        ],
        flops=2**31,
        vmem=20 * MIB,
    )
    input_blocks, lags_came = lax.optimization_barrier((input_blocks, lags_came))
    returned = lax.all_to_all(input_blocks, ("y", "w"), split_axis=0, concat_axis=0, tiled=True)
    shares = call(
        join_kernel,
        [jax.ShapeDtypeStruct((places, LANES), f32)] * SIDE,
        lags_came,
    )
    came = []
    for step in range(SIDE):
        moves = []
        for side in range(SIDE):
            for inner in range(SIDE):
                moves.append((side * SIDE + inner, inner * SIDE + (side + step) % SIDE))
        came.append(lax.ppermute(shares[step], ("zh", "w"), moves))
    scale = 1.0 / math.sqrt(GROUP * seqs * length)
    filter_part = call(
        lambda *refs: last_kernel(scale, *refs),
        jax.ShapeDtypeStruct((places, LANES), f32),
        *came,
    )
    input_grad = call(
        unpack_kernel, jax.ShapeDtypeStruct((tokens, width), bf16), returned, vmem=4 * MIB
    )
    return (input_grad[None], filter_part.T)


def solution(mesh):
    cut = Mesh(mesh.devices.reshape(SIDE, SIDE, -1, SIDE), ("x", "zh", "y", "w"))
    seq, token = ("x", "zh"), ("y", "w")
    in_specs = (P(seq, token, None), P(seq, token, None), P(token, None))
    out_specs = (P(seq, token, None), P(token, seq))
    return jax.shard_map(
        on_device, mesh=cut, in_specs=in_specs, out_specs=out_specs, check_vma=False
    )
```

```python
import math

import jax
import jax.numpy as jnp
from jax import lax
from jax.experimental import pallas as pl
from jax.experimental.pallas import tpu as pltpu
from jax.sharding import Mesh, PartitionSpec as P

GROUP = 16
LANES = 128
SPAN = 2 * LANES
SIDE = 4
MIB = 1024 * 1024
PACK_VMEM = 56 * MIB


def call(kernel, out_shape, *operands, scratch=(), flops=2**20, vmem=2 * MIB, space=pltpu.VMEM):
    whole = pl.BlockSpec(memory_space=space)
    several = isinstance(out_shape, (list, tuple))
    return pl.pallas_call(
        kernel,
        out_shape=out_shape,
        in_specs=[whole] * len(operands),
        out_specs=[whole] * len(out_shape) if several else whole,
        scratch_shapes=list(scratch),
        compiler_params=pltpu.CompilerParams(vmem_limit_bytes=vmem),
        cost_estimate=pl.CostEstimate(flops=flops, bytes_accessed=2**20, transcendentals=0),
    )(*operands)


def pack_kernel(
    saved_hbm, grad_hbm, filt_hbm, out_hbm, saved_ref, grad_ref, filt_ref, out_ref, lines_ref, sems
):
    places, groups = LANES // GROUP, SIDE
    channels = groups * GROUP
    width = SIDE * LANES
    filt_copy = pltpu.make_async_copy(filt_hbm, filt_ref, sems.at[0])
    filt_copy.start()
    copies = []
    for slot in range(groups):
        cols = pl.ds(slot * width, width)
        for kind, (source, target) in enumerate(((grad_hbm, grad_ref), (saved_hbm, saved_ref))):
            copy = pltpu.make_async_copy(
                source.at[:, cols], target.at[:, cols], sems.at[1 + 2 * slot + kind]
            )
            copy.start()
            copies.append(copy)
    filt_copy.wait()
    lines_ref[...] = filt_ref[...].astype(jnp.float32).T
    empty = jnp.zeros((out_ref.shape[2] - 2 * channels - groups, LANES), jnp.float32)
    for place in range(places):
        for inner in range(SIDE):
            first = inner * places + place
            mine = lines_ref[pl.ds(first, groups, stride=SIDE * places), :]
            block = jnp.concatenate([mine, empty], axis=0)
            out_ref[place, inner, 2 * channels :, :] = block.astype(jnp.bfloat16)
    for copy in copies:
        copy.wait()
    outs = []
    for inner in range(SIDE):
        for slot in range(groups):
            tile = slot * SIDE + inner
            cols = slice(tile * LANES, (tile + 1) * LANES)
            grad_rows = grad_ref[:, cols].T
            saved_rows = saved_ref[:, cols].T
            row = slot * GROUP
            for place in range(places):
                mine = slice(place * GROUP, (place + 1) * GROUP)
                out_ref[place, inner, row : row + GROUP, :] = grad_rows[mine, :]
                out_ref[place, inner, channels + row : channels + row + GROUP, :] = saved_rows[
                    mine, :
                ]
        copy = pltpu.make_async_copy(
            out_ref.at[:, inner], out_hbm.at[:, inner], sems.at[1 + 2 * groups + inner]
        )
        copy.start()
        outs.append(copy)
    for copy in outs:
        copy.wait()


def unpack_kernel(blocks_ref, out_ref):
    places = LANES // GROUP
    for tile in range(out_ref.shape[1] // LANES):
        slot, inner = tile // SIDE, tile % SIDE
        row = slot * GROUP
        rows = [
            blocks_ref[place * SIDE + inner, row : row + GROUP, :] for place in range(places)
        ]
        out_ref[:, tile * LANES : (tile + 1) * LANES] = jnp.concatenate(rows, axis=0).T


def widen_blocks(blocks_ref, first, wide_ref):
    for part in range(blocks_ref.shape[0]):
        row = (part // 2) * GROUP
        lane = (part % 2) * LANES
        wide_ref[row : row + GROUP, lane : lane + LANES] = blocks_ref[
            part, pl.ds(first, GROUP), :
        ]


def input_kernel(blocks_ref, out_ref, line_ref, wide_ref, toep_ref):
    parts, channels, _ = out_ref.shape
    groups = channels // GROUP
    half = parts // 2
    rows = half * GROUP
    wide_ref[rows:, :] = jnp.zeros_like(wide_ref[rows:, :])
    line_ref[...] = jnp.zeros_like(line_ref)
    for part in range(parts):
        start = (part + 1) * LANES
        line_ref[:, start : start + LANES] = blocks_ref[part, 2 * channels :, :][
            : line_ref.shape[0]
        ].astype(jnp.float32)

    def per_group(group, carry):
        first = pl.multiple_of(group * GROUP, GROUP)
        widen_blocks(blocks_ref, first, wide_ref)
        line = line_ref[pl.ds(group, 1), :]
        spread = jnp.broadcast_to(line, (LANES, line.shape[1]))
        toep_ref[...] = pltpu.roll(spread, 0, 1, stride=1, stride_axis=0).astype(jnp.bfloat16)
        total = jnp.zeros((rows, SPAN), jnp.float32)
        for lag in range(half):
            start = lag * SPAN
            taps = jnp.concatenate(
                [
                    toep_ref[:, start + LANES : start + LANES + SPAN],
                    toep_ref[:, start : start + SPAN],
                ],
                axis=0,
            )
            total = total + lax.dot_general(
                wide_ref[lag * GROUP : lag * GROUP + rows, :],
                taps,
                (((1,), (1,)), ((), ())),
                preferred_element_type=jnp.float32,
            )
        done = total.astype(jnp.bfloat16)
        for part in range(parts):
            row = (part // 2) * GROUP
            lane = (part % 2) * LANES
            out_ref[part, pl.ds(first, GROUP), :] = done[
                row : row + GROUP, lane : lane + LANES
            ]
        return carry

    lax.fori_loop(0, groups, per_group, 0)


def filter_kernel(blocks_ref, out_ref, tall_ref, saved_ref, product_ref):
    parts = blocks_ref.shape[0]
    rows = parts * GROUP
    groups = SIDE
    channels = groups * GROUP
    row_ids = lax.broadcasted_iota(jnp.int32, (LANES, LANES), 0)
    col_ids = lax.broadcasted_iota(jnp.int32, (LANES, LANES), 1)
    flip = jnp.where(row_ids + col_ids == LANES - 1, 1.0, 0.0).astype(jnp.bfloat16)
    empty = jnp.zeros((LANES, LANES), jnp.float32)
    product_ref[:, :LANES] = empty
    product_ref[:, (parts + 1) * LANES :] = empty
    tall_ref[rows - GROUP :, LANES:] = jnp.zeros((GROUP, LANES), jnp.bfloat16)
    for group in range(groups):
        first = group * GROUP
        for part in range(parts):
            mine = blocks_ref[part, first : first + GROUP, :]
            here = slice(part * GROUP, (part + 1) * GROUP)
            tall_ref[here, :LANES] = mine
            if part > 0:
                tall_ref[(part - 1) * GROUP : part * GROUP, LANES:] = mine
            saved_ref[here, :] = blocks_ref[part, channels + first : channels + first + GROUP, :]
        flipped = lax.dot_general(
            flip, saved_ref[...], (((1,), (1,)), ((), ())), preferred_element_type=jnp.float32
        ).astype(jnp.bfloat16)
        for pair in range(parts // 2):
            start = 2 * pair * GROUP
            depth = rows - start
            product_ref[:, LANES + pair * SPAN : LANES + (pair + 1) * SPAN] = jnp.dot(
                flipped[:, :depth], tall_ref[start:, :], preferred_element_type=jnp.float32
            )
        turned = pltpu.roll(product_ref[...], 1, 1, stride=1, stride_axis=0)
        line = jnp.sum(turned, axis=0, keepdims=True)
        for part in range(parts):
            start = SPAN + part * LANES
            out_ref[group * parts + part] = line[:, start : start + LANES]


def split_kernel(came_ref, keep_ref, send_ref, total_ref):
    parts = came_ref.shape[0] // SIDE
    places = parts // SIDE
    total = came_ref[:parts]
    for step in range(1, SIDE):
        total = total + came_ref[step * parts : (step + 1) * parts]
    total_ref[...] = total.reshape(parts, LANES)
    half = lax.axis_index("zh") // 2
    for low in range(2):
        here = slice(low * places, (low + 1) * places)
        mine, other = 2 * half + low, 2 * (1 - half) + low
        keep_ref[here, :] = total_ref[pl.ds(mine, places, stride=SIDE), :]
        send_ref[here, :] = total_ref[pl.ds(other, places, stride=SIDE), :]


def halve_kernel(kept_ref, came_ref, keep_ref, send_ref, total_ref):
    places = keep_ref.shape[0]
    total_ref[...] = kept_ref[...] + came_ref[...]
    half = lax.axis_index("zh") % 2
    keep_ref[...] = total_ref[pl.ds(pl.multiple_of(half * places, places), places), :]
    send_ref[...] = total_ref[pl.ds(pl.multiple_of((1 - half) * places, places), places), :]


def last_kernel(scale, kept_ref, came_ref, out_ref):
    out_ref[...] = (kept_ref[...] + came_ref[...]) * scale


def on_device(u_saved, grad_out, filters):
    tokens, width = u_saved.shape[1:]
    parts = lax.axis_size(("y", "w"))
    seqs = lax.axis_size(("x", "zh"))
    places = lax.axis_size("y")
    channels = width // parts
    groups = channels // GROUP
    length = parts * LANES
    bf16, f32 = jnp.bfloat16, jnp.float32
    half_rows = parts // 2 * GROUP

    rows = 2 * channels + 8
    packed = call(
        pack_kernel,
        jax.ShapeDtypeStruct((places, SIDE, rows, LANES), bf16),
        u_saved[0],
        grad_out[0],
        filters,
        scratch=[
            pltpu.VMEM((tokens, width), bf16),
            pltpu.VMEM((tokens, width), bf16),
            pltpu.VMEM(filters.shape, bf16),
            pltpu.VMEM((places, SIDE, rows, LANES), bf16),
            pltpu.VMEM((LANES, LANES), f32),
            pltpu.SemaphoreType.DMA((1 + 2 * groups + SIDE,)),
        ],
        vmem=PACK_VMEM,
        space=pl.ANY,
    ).reshape(parts, rows, LANES)
    blocks = lax.all_to_all(packed, ("y", "w"), split_axis=0, concat_axis=0, tiled=True)
    lags = call(
        filter_kernel,
        jax.ShapeDtypeStruct((SIDE * parts, 1, LANES), f32),
        blocks,
        scratch=[
            pltpu.VMEM((2 * half_rows, SPAN), bf16),
            pltpu.VMEM((2 * half_rows, LANES), bf16),
            pltpu.VMEM((LANES, length + SPAN), f32),
        ],
        flops=2**31,
        vmem=20 * MIB,
    )
    lags_came = lax.all_to_all(lags, ("x", "y", "w"), split_axis=0, concat_axis=0, tiled=True)
    input_blocks = call(
        input_kernel,
        jax.ShapeDtypeStruct((parts, channels, LANES), bf16),
        blocks,
        scratch=[
            pltpu.VMEM((groups, length + SPAN), f32),
            pltpu.VMEM((2 * half_rows, SPAN), bf16),
            pltpu.VMEM((LANES, length + SPAN), bf16),
        ],
        flops=2**31,
        vmem=20 * MIB,
    )
    input_blocks, lags_came = lax.optimization_barrier((input_blocks, lags_came))
    returned = lax.all_to_all(input_blocks, ("y", "w"), split_axis=0, concat_axis=0, tiled=True)
    halves = [jax.ShapeDtypeStruct((2 * places, LANES), f32)] * 2
    whole_places = jax.ShapeDtypeStruct((places, LANES), f32)
    kept, sent = call(split_kernel, halves, lags_came, scratch=[pltpu.VMEM((parts, LANES), f32)])
    far = lax.ppermute(sent, "zh", [(side, side ^ 2) for side in range(SIDE)])
    kept, sent = call(
        halve_kernel,
        [whole_places] * 2,
        kept,
        far,
        scratch=[pltpu.VMEM((2 * places, LANES), f32)],
    )
    near = lax.ppermute(sent, "zh", [(side, side ^ 1) for side in range(SIDE)])
    input_grad = call(
        unpack_kernel, jax.ShapeDtypeStruct((tokens, width), bf16), returned, vmem=4 * MIB
    )
    scale = 1.0 / math.sqrt(GROUP * seqs * length)
    input_grad, near = lax.optimization_barrier((input_grad, near))
    filter_part = call(lambda *refs: last_kernel(scale, *refs), whole_places, kept, near)
    return (input_grad[None], filter_part.T)


def solution(mesh):
    cut = Mesh(mesh.devices.reshape(SIDE, SIDE, -1, SIDE), ("x", "zh", "y", "w"))
    seq, token = ("x", "zh"), ("y", "w")
    in_specs = (P(seq, token, None), P(seq, token, None), P(token, None))
    out_specs = (P(seq, token, None), P(token, seq))
    return jax.shard_map(
        on_device, mesh=cut, in_specs=in_specs, out_specs=out_specs, check_vma=False
    )
```

```python
import math

import jax
import jax.numpy as jnp
from jax import lax
from jax.experimental import pallas as pl
from jax.experimental.pallas import tpu as pltpu
from jax.sharding import Mesh, PartitionSpec as P

GROUP = 16
LANES = 128
SPAN = 2 * LANES
SIDE = 4
MIB = 1024 * 1024


def call(kernel, out_shape, *operands, scratch=(), flops=2**20, vmem=2 * MIB, space=pltpu.VMEM):
    given = pl.BlockSpec(memory_space=space)
    whole = pl.BlockSpec(memory_space=pltpu.VMEM)
    several = isinstance(out_shape, (list, tuple))
    return pl.pallas_call(
        kernel,
        out_shape=out_shape,
        in_specs=[given] * len(operands),
        out_specs=[whole] * len(out_shape) if several else whole,
        scratch_shapes=list(scratch),
        compiler_params=pltpu.CompilerParams(vmem_limit_bytes=vmem),
        cost_estimate=pl.CostEstimate(flops=flops, bytes_accessed=2**20, transcendentals=0),
    )(*operands)


def pack_kernel(
    saved_hbm, grad_hbm, filt_hbm, out_ref, saved_ref, grad_ref, filt_ref, lines_ref, sems
):
    places, groups = LANES // GROUP, SIDE
    channels = groups * GROUP
    filt_copy = pltpu.make_async_copy(filt_hbm, filt_ref, sems.at[0])
    filt_copy.start()
    grad_copy = pltpu.make_async_copy(grad_hbm, grad_ref, sems.at[1])
    saved_copy = pltpu.make_async_copy(saved_hbm, saved_ref, sems.at[2])
    grad_copy.start()
    saved_copy.start()
    filt_copy.wait()
    lines_ref[...] = filt_ref[...].astype(jnp.float32).T
    empty = jnp.zeros((out_ref.shape[2] - 2 * channels - groups, LANES), jnp.float32)
    for place in range(places):
        for inner in range(SIDE):
            first = inner * places + place
            mine = lines_ref[pl.ds(first, groups, stride=SIDE * places), :]
            block = jnp.concatenate([mine, empty], axis=0)
            out_ref[place, inner, 2 * channels :, :] = block.astype(jnp.bfloat16)
    grad_copy.wait()
    saved_copy.wait()
    for tile in range(groups * SIDE):
        slot, inner = tile // SIDE, tile % SIDE
        cols = slice(tile * LANES, (tile + 1) * LANES)
        grad_rows = grad_ref[:, cols].T
        saved_rows = saved_ref[:, cols].T
        row = slot * GROUP
        for place in range(places):
            mine = slice(place * GROUP, (place + 1) * GROUP)
            out_ref[place, inner, row : row + GROUP, :] = grad_rows[mine, :]
            out_ref[place, inner, channels + row : channels + row + GROUP, :] = saved_rows[mine, :]


def widen_blocks(blocks_ref, first, wide_ref):
    for part in range(blocks_ref.shape[0]):
        row = (part // 2) * GROUP
        lane = (part % 2) * LANES
        wide_ref[row : row + GROUP, lane : lane + LANES] = blocks_ref[
            part, first : first + GROUP, :
        ]


def input_kernel(blocks_ref, out_ref, line_ref, wide_refs, toep_refs):
    parts, channels, _ = out_ref.shape
    groups = channels // GROUP
    half = parts // 2
    rows = half * GROUP
    slots = wide_refs.shape[0]
    for slot in range(slots):
        wide_refs[slot, rows:, :] = jnp.zeros((rows, SPAN), jnp.bfloat16)
    line_ref[...] = jnp.zeros_like(line_ref)
    for part in range(parts):
        start = (part + 1) * LANES
        line_ref[:, start : start + LANES] = blocks_ref[part, 2 * channels :, :][:groups].astype(
            jnp.float32
        )

    def prepare(group):
        slot = group % slots
        widen_blocks(blocks_ref, group * GROUP, wide_refs.at[slot])
        line = line_ref[group : group + 1, :]
        spread = jnp.broadcast_to(line, (LANES, line.shape[1]))
        toep_refs[slot] = pltpu.roll(spread, 0, 1, stride=1, stride_axis=0).astype(jnp.bfloat16)

    def multiply(group):
        slot = group % slots
        total = jnp.zeros((rows, SPAN), jnp.float32)
        for lag in range(half):
            start = lag * SPAN
            taps = jnp.concatenate(
                [
                    toep_refs[slot, :, start + LANES : start + LANES + SPAN],
                    toep_refs[slot, :, start : start + SPAN],
                ],
                axis=0,
            )
            total = total + lax.dot_general(
                wide_refs[slot, lag * GROUP : lag * GROUP + rows, :],
                taps,
                (((1,), (1,)), ((), ())),
                preferred_element_type=jnp.float32,
            )
        done = total.astype(jnp.bfloat16)
        first = group * GROUP
        for part in range(parts):
            row = (part // 2) * GROUP
            lane = (part % 2) * LANES
            out_ref[part, first : first + GROUP, :] = done[row : row + GROUP, lane : lane + LANES]

    prepare(0)
    for group in range(groups):
        if group + 1 < groups:
            prepare(group + 1)
        multiply(group)


def filter_kernel(blocks_ref, out_ref, tall_ref, saved_ref, product_ref):
    parts = blocks_ref.shape[0]
    rows = parts * GROUP
    groups = SIDE
    channels = groups * GROUP
    row_ids = lax.broadcasted_iota(jnp.int32, (LANES, LANES), 0)
    col_ids = lax.broadcasted_iota(jnp.int32, (LANES, LANES), 1)
    flip = jnp.where(row_ids + col_ids == LANES - 1, 1.0, 0.0).astype(jnp.bfloat16)
    empty = jnp.zeros((LANES, LANES), jnp.float32)
    product_ref[:, :LANES] = empty
    product_ref[:, (parts + 1) * LANES :] = empty
    tall_ref[rows - GROUP :, LANES:] = jnp.zeros((GROUP, LANES), jnp.bfloat16)
    for group in range(groups):
        first = group * GROUP
        for part in range(parts):
            mine = blocks_ref[part, first : first + GROUP, :]
            here = slice(part * GROUP, (part + 1) * GROUP)
            tall_ref[here, :LANES] = mine
            if part > 0:
                tall_ref[(part - 1) * GROUP : part * GROUP, LANES:] = mine
            saved_ref[here, :] = blocks_ref[part, channels + first : channels + first + GROUP, :]
        flipped = lax.dot_general(
            flip, saved_ref[...], (((1,), (1,)), ((), ())), preferred_element_type=jnp.float32
        ).astype(jnp.bfloat16)
        for pair in range(parts // 2):
            start = 2 * pair * GROUP
            depth = rows - start
            product_ref[:, LANES + pair * SPAN : LANES + (pair + 1) * SPAN] = jnp.dot(
                flipped[:, :depth], tall_ref[start:, :], preferred_element_type=jnp.float32
            )
        turned = pltpu.roll(product_ref[...], 1, 1, stride=1, stride_axis=0)
        line = jnp.sum(turned, axis=0, keepdims=True)
        for part in range(parts):
            start = SPAN + part * LANES
            out_ref[group * parts + part] = line[:, start : start + LANES]


def split_kernel(came_ref, keep_ref, send_ref, total_ref):
    parts = came_ref.shape[0] // SIDE
    places = parts // SIDE
    total = came_ref[:parts]
    for step in range(1, SIDE):
        total = total + came_ref[step * parts : (step + 1) * parts]
    total_ref[...] = total.reshape(parts, LANES)
    half = lax.axis_index("zh") // 2
    for low in range(2):
        here = slice(low * places, (low + 1) * places)
        mine, other = 2 * half + low, 2 * (1 - half) + low
        keep_ref[here, :] = total_ref[pl.ds(mine, places, stride=SIDE), :]
        send_ref[here, :] = total_ref[pl.ds(other, places, stride=SIDE), :]


def halve_kernel(kept_ref, came_ref, keep_ref, send_ref, total_ref):
    places = keep_ref.shape[0]
    total_ref[...] = kept_ref[...] + came_ref[...]
    half = lax.axis_index("zh") % 2
    keep_ref[...] = total_ref[pl.ds(pl.multiple_of(half * places, places), places), :]
    send_ref[...] = total_ref[pl.ds(pl.multiple_of((1 - half) * places, places), places), :]


def last_kernel(scale, blocks_ref, kept_ref, came_ref, input_ref, filter_ref):
    filter_ref[...] = (kept_ref[...] + came_ref[...]) * scale
    places = LANES // GROUP
    for tile in range(input_ref.shape[1] // LANES):
        slot, inner = tile // SIDE, tile % SIDE
        row = slot * GROUP
        rows = [
            blocks_ref[place * SIDE + inner, row : row + GROUP, :] for place in range(places)
        ]
        input_ref[:, tile * LANES : (tile + 1) * LANES] = jnp.concatenate(rows, axis=0).T


def on_device(u_saved, grad_out, filters):
    tokens, width = u_saved.shape[1:]
    parts = lax.axis_size(("y", "w"))
    seqs = lax.axis_size(("x", "zh"))
    places = lax.axis_size("y")
    channels = width // parts
    groups = channels // GROUP
    length = parts * LANES
    bf16, f32 = jnp.bfloat16, jnp.float32
    half_rows = parts // 2 * GROUP

    rows = 2 * channels + 8
    packed = call(
        pack_kernel,
        jax.ShapeDtypeStruct((places, SIDE, rows, LANES), bf16),
        *(
            pltpu.with_memory_space_constraint(array, pltpu.HBM)
            for array in (u_saved[0], grad_out[0], filters)
        ),
        scratch=[
            pltpu.VMEM((tokens, width), bf16),
            pltpu.VMEM((tokens, width), bf16),
            pltpu.VMEM(filters.shape, bf16),
            pltpu.VMEM((LANES, LANES), f32),
            pltpu.SemaphoreType.DMA((3,)),
        ],
        vmem=8 * MIB,
        space=pltpu.HBM,
    ).reshape(parts, rows, LANES)
    blocks = lax.all_to_all(packed, ("y", "w"), split_axis=0, concat_axis=0, tiled=True)
    lags = call(
        filter_kernel,
        jax.ShapeDtypeStruct((SIDE * parts, 1, LANES), f32),
        blocks,
        scratch=[
            pltpu.VMEM((2 * half_rows, SPAN), bf16),
            pltpu.VMEM((2 * half_rows, LANES), bf16),
            pltpu.VMEM((LANES, length + SPAN), f32),
        ],
        flops=2**31,
        vmem=20 * MIB,
    )
    lags_came = lax.all_to_all(lags, ("x", "y", "w"), split_axis=0, concat_axis=0, tiled=True)
    input_blocks = call(
        input_kernel,
        jax.ShapeDtypeStruct((parts, channels, LANES), bf16),
        blocks,
        scratch=[
            pltpu.VMEM((groups, length + SPAN), f32),
            pltpu.VMEM((2, 2 * half_rows, SPAN), bf16),
            pltpu.VMEM((2, LANES, length + SPAN), bf16),
        ],
        flops=2**31,
        vmem=20 * MIB,
    )
    input_blocks, lags_came = lax.optimization_barrier((input_blocks, lags_came))
    returned = lax.all_to_all(input_blocks, ("y", "w"), split_axis=0, concat_axis=0, tiled=True)
    halves = [jax.ShapeDtypeStruct((2 * places, LANES), f32)] * 2
    whole_places = jax.ShapeDtypeStruct((places, LANES), f32)
    kept, sent = call(split_kernel, halves, lags_came, scratch=[pltpu.VMEM((parts, LANES), f32)])
    far = lax.ppermute(sent, "zh", [(side, side ^ 2) for side in range(SIDE)])
    kept, sent = call(
        halve_kernel,
        [whole_places] * 2,
        kept,
        far,
        scratch=[pltpu.VMEM((2 * places, LANES), f32)],
    )
    near = lax.ppermute(sent, "zh", [(side, side ^ 1) for side in range(SIDE)])
    scale = 1.0 / math.sqrt(GROUP * seqs * length)
    input_grad, filter_part = call(
        lambda *refs: last_kernel(scale, *refs),
        [jax.ShapeDtypeStruct((tokens, width), bf16), whole_places],
        returned,
        kept,
        near,
        vmem=4 * MIB,
    )
    return (input_grad[None], filter_part.T)


def solution(mesh):
    cut = Mesh(mesh.devices.reshape(SIDE, SIDE, -1, SIDE), ("x", "zh", "y", "w"))
    seq, token = ("x", "zh"), ("y", "w")
    in_specs = (P(seq, token, None), P(seq, token, None), P(token, None))
    out_specs = (P(seq, token, None), P(token, seq))
    return jax.shard_map(
        on_device, mesh=cut, in_specs=in_specs, out_specs=out_specs, check_vma=False
    )
```

```python
import math

import jax
import jax.numpy as jnp
from jax import lax
from jax.experimental import pallas as pl
from jax.experimental.pallas import tpu as pltpu
from jax.sharding import Mesh, PartitionSpec as P

GROUP = 16
LANES = 128
SPAN = 2 * LANES
SIDE = 4
MIB = 1024 * 1024


def call(kernel, out_shape, *operands, scratch=(), flops=2**20, vmem=2 * MIB, space=pltpu.VMEM):
    given = pl.BlockSpec(memory_space=space)
    whole = pl.BlockSpec(memory_space=pltpu.VMEM)
    several = isinstance(out_shape, (list, tuple))
    return pl.pallas_call(
        kernel,
        out_shape=out_shape,
        in_specs=[given] * len(operands),
        out_specs=[whole] * len(out_shape) if several else whole,
        scratch_shapes=list(scratch),
        compiler_params=pltpu.CompilerParams(vmem_limit_bytes=vmem),
        cost_estimate=pl.CostEstimate(flops=flops, bytes_accessed=2**20, transcendentals=0),
    )(*operands)


def pack_kernel(
    saved_hbm, grad_hbm, filt_hbm, out_ref, saved_ref, grad_ref, filt_ref, lines_ref, sems
):
    places, groups = LANES // GROUP, SIDE
    channels = groups * GROUP
    filt_copy = pltpu.make_async_copy(filt_hbm, filt_ref, sems.at[0])
    filt_copy.start()
    grad_copy = pltpu.make_async_copy(grad_hbm, grad_ref, sems.at[1])
    saved_copy = pltpu.make_async_copy(saved_hbm, saved_ref, sems.at[2])
    grad_copy.start()
    saved_copy.start()
    filt_copy.wait()
    lines_ref[...] = filt_ref[...].astype(jnp.float32).T
    empty = jnp.zeros((out_ref.shape[2] - 2 * channels - groups, LANES), jnp.float32)
    for place in range(places):
        for inner in range(SIDE):
            first = inner * places + place
            mine = lines_ref[pl.ds(first, groups, stride=SIDE * places), :]
            block = jnp.concatenate([mine, empty], axis=0)
            out_ref[place, inner, 2 * channels :, :] = block.astype(jnp.bfloat16)
    grad_copy.wait()
    saved_copy.wait()
    for tile in range(groups * SIDE):
        slot, inner = tile // SIDE, tile % SIDE
        cols = slice(tile * LANES, (tile + 1) * LANES)
        grad_rows = grad_ref[:, cols].T
        saved_rows = saved_ref[:, cols].T
        row = slot * GROUP
        for place in range(places):
            mine = slice(place * GROUP, (place + 1) * GROUP)
            out_ref[place, inner, row : row + GROUP, :] = grad_rows[mine, :]
            out_ref[place, inner, channels + row : channels + row + GROUP, :] = saved_rows[mine, :]


def widen_blocks(blocks_ref, first, wide_ref):
    for part in range(blocks_ref.shape[0]):
        row = (part // 2) * GROUP
        lane = (part % 2) * LANES
        wide_ref[row : row + GROUP, lane : lane + LANES] = blocks_ref[
            part, first : first + GROUP, :
        ]


def input_kernel(blocks_ref, out_ref, line_ref, wide_refs, toep_refs):
    parts, channels, _ = out_ref.shape
    groups = channels // GROUP
    half = parts // 2
    rows = half * GROUP
    slots = wide_refs.shape[0]
    for slot in range(slots):
        wide_refs[slot, rows:, :] = jnp.zeros((rows, SPAN), jnp.bfloat16)
    line_ref[...] = jnp.zeros_like(line_ref)
    for part in range(parts):
        start = (part + 1) * LANES
        line_ref[:, start : start + LANES] = blocks_ref[part, 2 * channels :, :][:groups].astype(
            jnp.float32
        )

    def prepare(group):
        slot = group % slots
        widen_blocks(blocks_ref, group * GROUP, wide_refs.at[slot])
        line = line_ref[group : group + 1, :]
        spread = jnp.broadcast_to(line, (LANES, line.shape[1]))
        toep_refs[slot] = pltpu.roll(spread, 0, 1, stride=1, stride_axis=0).astype(jnp.bfloat16)

    def multiply(group):
        slot = group % slots
        total = jnp.zeros((rows, SPAN), jnp.float32)
        for lag in range(half):
            start = lag * SPAN
            taps = jnp.concatenate(
                [
                    toep_refs[slot, :, start + LANES : start + LANES + SPAN],
                    toep_refs[slot, :, start : start + SPAN],
                ],
                axis=0,
            )
            total = total + lax.dot_general(
                wide_refs[slot, lag * GROUP : lag * GROUP + rows, :],
                taps,
                (((1,), (1,)), ((), ())),
                preferred_element_type=jnp.float32,
            )
        done = total.astype(jnp.bfloat16)
        first = group * GROUP
        for part in range(parts):
            row = (part // 2) * GROUP
            lane = (part % 2) * LANES
            out_ref[part, first : first + GROUP, :] = done[row : row + GROUP, lane : lane + LANES]

    prepare(0)
    for group in range(groups):
        if group + 1 < groups:
            prepare(group + 1)
        multiply(group)


def filter_kernel(blocks_ref, out_ref, tall_refs, saved_ref, product_refs):
    parts = blocks_ref.shape[0]
    rows = parts * GROUP
    groups = SIDE
    channels = groups * GROUP
    row_ids = lax.broadcasted_iota(jnp.int32, (LANES, LANES), 0)
    col_ids = lax.broadcasted_iota(jnp.int32, (LANES, LANES), 1)
    flip = jnp.where(row_ids + col_ids == LANES - 1, 1.0, 0.0).astype(jnp.bfloat16)
    empty = jnp.zeros((LANES, LANES), jnp.float32)
    for group in range(groups):
        product_refs[group, :, :LANES] = empty
        product_refs[group, :, (parts + 1) * LANES :] = empty
        tall_refs[group, rows - GROUP :, LANES:] = jnp.zeros((GROUP, LANES), jnp.bfloat16)

    def multiply(group):
        first = group * GROUP
        tall_ref, product_ref = tall_refs.at[group], product_refs.at[group]
        for part in range(parts):
            mine = blocks_ref[part, first : first + GROUP, :]
            here = slice(part * GROUP, (part + 1) * GROUP)
            tall_ref[here, :LANES] = mine
            if part > 0:
                tall_ref[(part - 1) * GROUP : part * GROUP, LANES:] = mine
            saved_ref[group, here, :] = blocks_ref[
                part, channels + first : channels + first + GROUP, :
            ]
        flipped = lax.dot_general(
            flip, saved_ref[group], (((1,), (1,)), ((), ())), preferred_element_type=jnp.float32
        ).astype(jnp.bfloat16)
        for pair in range(parts // 2):
            start = 2 * pair * GROUP
            depth = rows - start
            product_ref[:, LANES + pair * SPAN : LANES + (pair + 1) * SPAN] = jnp.dot(
                flipped[:, :depth], tall_ref[start:, :], preferred_element_type=jnp.float32
            )

    def add_up(group):
        turned = pltpu.roll(product_refs[group], 1, 1, stride=1, stride_axis=0)
        line = jnp.sum(turned, axis=0, keepdims=True)
        for part in range(parts):
            start = SPAN + part * LANES
            out_ref[group * parts + part] = line[:, start : start + LANES]

    for group in range(groups):
        multiply(group)
        if group > 0:
            add_up(group - 1)
    add_up(groups - 1)


def split_kernel(came_ref, keep_ref, send_ref, total_ref):
    parts = came_ref.shape[0] // SIDE
    places = parts // SIDE
    total = came_ref[:parts]
    for step in range(1, SIDE):
        total = total + came_ref[step * parts : (step + 1) * parts]
    total_ref[...] = total.reshape(parts, LANES)
    half = lax.rem(lax.axis_index("zh"), 2)
    for low in range(2):
        here = slice(low * places, (low + 1) * places)
        mine, other = 2 * low + half, 2 * low + 1 - half
        keep_ref[here, :] = total_ref[pl.ds(mine, places, stride=SIDE), :]
        send_ref[here, :] = total_ref[pl.ds(other, places, stride=SIDE), :]


def halve_kernel(kept_ref, came_ref, keep_ref, send_ref, total_ref):
    places = keep_ref.shape[0]
    total_ref[...] = kept_ref[...] + came_ref[...]
    half = lax.axis_index("zh") // 2
    keep_ref[...] = total_ref[pl.ds(pl.multiple_of(half * places, places), places), :]
    send_ref[...] = total_ref[pl.ds(pl.multiple_of((1 - half) * places, places), places), :]


def last_kernel(scale, blocks_ref, kept_ref, came_ref, input_ref, filter_ref):
    filter_ref[...] = (kept_ref[...] + came_ref[...]) * scale
    places = LANES // GROUP
    for tile in range(input_ref.shape[1] // LANES):
        slot, inner = tile // SIDE, tile % SIDE
        row = slot * GROUP
        rows = [
            blocks_ref[place * SIDE + inner, row : row + GROUP, :] for place in range(places)
        ]
        input_ref[:, tile * LANES : (tile + 1) * LANES] = jnp.concatenate(rows, axis=0).T


def on_device(u_saved, grad_out, filters):
    tokens, width = u_saved.shape[1:]
    parts = lax.axis_size(("y", "w"))
    seqs = lax.axis_size(("x", "zh"))
    places = lax.axis_size("y")
    channels = width // parts
    groups = channels // GROUP
    length = parts * LANES
    bf16, f32 = jnp.bfloat16, jnp.float32
    half_rows = parts // 2 * GROUP

    rows = 2 * channels + 8
    packed = call(
        pack_kernel,
        jax.ShapeDtypeStruct((places, SIDE, rows, LANES), bf16),
        *(
            pltpu.with_memory_space_constraint(array, pltpu.HBM)
            for array in (u_saved[0], grad_out[0], filters)
        ),
        scratch=[
            pltpu.VMEM((tokens, width), bf16),
            pltpu.VMEM((tokens, width), bf16),
            pltpu.VMEM(filters.shape, bf16),
            pltpu.VMEM((LANES, LANES), f32),
            pltpu.SemaphoreType.DMA((3,)),
        ],
        vmem=8 * MIB,
        space=pltpu.HBM,
    ).reshape(parts, rows, LANES)
    blocks = lax.all_to_all(packed, ("y", "w"), split_axis=0, concat_axis=0, tiled=True)
    lags = call(
        filter_kernel,
        jax.ShapeDtypeStruct((SIDE * parts, 1, LANES), f32),
        blocks,
        scratch=[
            pltpu.VMEM((groups, 2 * half_rows, SPAN), bf16),
            pltpu.VMEM((groups, 2 * half_rows, LANES), bf16),
            pltpu.VMEM((groups, LANES, length + SPAN), f32),
        ],
        flops=2**31,
        vmem=24 * MIB,
    )
    lags_came = lax.all_to_all(lags, ("x", "y", "w"), split_axis=0, concat_axis=0, tiled=True)
    input_blocks = call(
        input_kernel,
        jax.ShapeDtypeStruct((parts, channels, LANES), bf16),
        blocks,
        scratch=[
            pltpu.VMEM((groups, length + SPAN), f32),
            pltpu.VMEM((2, 2 * half_rows, SPAN), bf16),
            pltpu.VMEM((2, LANES, length + SPAN), bf16),
        ],
        flops=2**31,
        vmem=20 * MIB,
    )
    input_blocks, lags_came = lax.optimization_barrier((input_blocks, lags_came))
    returned = lax.all_to_all(input_blocks, ("y", "w"), split_axis=0, concat_axis=0, tiled=True)
    halves = [jax.ShapeDtypeStruct((2 * places, LANES), f32)] * 2
    whole_places = jax.ShapeDtypeStruct((places, LANES), f32)
    kept, sent = call(split_kernel, halves, lags_came, scratch=[pltpu.VMEM((parts, LANES), f32)])
    close = lax.ppermute(sent, "zh", [(side, side ^ 1) for side in range(SIDE)])
    kept, sent = call(
        halve_kernel,
        [whole_places] * 2,
        kept,
        close,
        scratch=[pltpu.VMEM((2 * places, LANES), f32)],
    )
    distant = lax.ppermute(sent, "zh", [(side, side ^ 2) for side in range(SIDE)])
    scale = 1.0 / math.sqrt(GROUP * seqs * length)
    input_grad, filter_part = call(
        lambda *refs: last_kernel(scale, *refs),
        [jax.ShapeDtypeStruct((tokens, width), bf16), whole_places],
        returned,
        kept,
        distant,
        vmem=4 * MIB,
    )
    return (input_grad[None], filter_part.T)


def solution(mesh):
    cut = Mesh(mesh.devices.reshape(SIDE, SIDE, -1, SIDE), ("x", "zh", "y", "w"))
    seq, token = ("x", "zh"), ("y", "w")
    in_specs = (P(seq, token, None), P(seq, token, None), P(token, None))
    out_specs = (P(seq, token, None), P(token, seq))
    return jax.shard_map(
        on_device, mesh=cut, in_specs=in_specs, out_specs=out_specs, check_vma=False
    )
```

```python
import math

import jax
import jax.numpy as jnp
from jax import lax
from jax.experimental import pallas as pl
from jax.experimental.pallas import tpu as pltpu
from jax.sharding import Mesh, PartitionSpec as P

GROUP = 16
LANES = 128
SPAN = 2 * LANES
SIDE = 4
MIB = 1024 * 1024


def call(kernel, out_shape, *operands, scratch=(), flops=2**20, vmem=2 * MIB, space=pltpu.VMEM):
    given = pl.BlockSpec(memory_space=space)
    whole = pl.BlockSpec(memory_space=pltpu.VMEM)
    several = isinstance(out_shape, (list, tuple))
    return pl.pallas_call(
        kernel,
        out_shape=out_shape,
        in_specs=[given] * len(operands),
        out_specs=[whole] * len(out_shape) if several else whole,
        scratch_shapes=list(scratch),
        compiler_params=pltpu.CompilerParams(vmem_limit_bytes=vmem),
        cost_estimate=pl.CostEstimate(flops=flops, bytes_accessed=2**20, transcendentals=0),
    )(*operands)


def pack_kernel(
    saved_hbm, grad_hbm, filt_hbm, out_ref, saved_ref, grad_ref, filt_ref, lines_ref, sems
):
    places, groups = LANES // GROUP, SIDE
    channels = groups * GROUP
    filt_copy = pltpu.make_async_copy(filt_hbm, filt_ref, sems.at[0])
    filt_copy.start()
    grad_copy = pltpu.make_async_copy(grad_hbm, grad_ref, sems.at[1])
    saved_copy = pltpu.make_async_copy(saved_hbm, saved_ref, sems.at[2])
    grad_copy.start()
    saved_copy.start()
    filt_copy.wait()
    lines_ref[...] = filt_ref[...].astype(jnp.float32).T
    empty = jnp.zeros((out_ref.shape[2] - 2 * channels - groups, LANES), jnp.float32)
    for place in range(places):
        for inner in range(SIDE):
            first = inner * places + place
            mine = lines_ref[pl.ds(first, groups, stride=SIDE * places), :]
            block = jnp.concatenate([mine, empty], axis=0)
            out_ref[place, inner, 2 * channels :, :] = block.astype(jnp.bfloat16)
    grad_copy.wait()
    saved_copy.wait()
    for tile in range(groups * SIDE):
        slot, inner = tile // SIDE, tile % SIDE
        cols = slice(tile * LANES, (tile + 1) * LANES)
        grad_rows = grad_ref[:, cols].T
        saved_rows = saved_ref[:, cols].T
        row = slot * GROUP
        for place in range(places):
            mine = slice(place * GROUP, (place + 1) * GROUP)
            out_ref[place, inner, row : row + GROUP, :] = grad_rows[mine, :]
            out_ref[place, inner, channels + row : channels + row + GROUP, :] = saved_rows[mine, :]


def widen_blocks(blocks_ref, first, wide_ref):
    for part in range(blocks_ref.shape[0]):
        row = (part // 2) * GROUP
        lane = (part % 2) * LANES
        wide_ref[row : row + GROUP, lane : lane + LANES] = blocks_ref[
            part, first : first + GROUP, :
        ]


def input_kernel(blocks_ref, out_ref, line_ref, wide_refs, toep_refs):
    parts, channels, _ = out_ref.shape
    groups = channels // GROUP
    half = parts // 2
    rows = half * GROUP
    slots = wide_refs.shape[0]
    for slot in range(slots):
        wide_refs[slot, rows:, :] = jnp.zeros((rows, SPAN), jnp.bfloat16)
    line_ref[...] = jnp.zeros_like(line_ref)
    for part in range(parts):
        start = (part + 1) * LANES
        line_ref[:, start : start + LANES] = blocks_ref[part, 2 * channels :, :][:groups].astype(
            jnp.float32
        )

    def prepare(group):
        slot = group % slots
        widen_blocks(blocks_ref, group * GROUP, wide_refs.at[slot])
        line = line_ref[group : group + 1, :]
        spread = jnp.broadcast_to(line, (LANES, line.shape[1]))
        toep_refs[slot] = pltpu.roll(spread, 0, 1, stride=1, stride_axis=0).astype(jnp.bfloat16)

    def multiply(group):
        slot = group % slots
        total = jnp.zeros((rows, SPAN), jnp.float32)
        for lag in range(half):
            start = lag * SPAN
            taps = jnp.concatenate(
                [
                    toep_refs[slot, :, start + LANES : start + LANES + SPAN],
                    toep_refs[slot, :, start : start + SPAN],
                ],
                axis=0,
            )
            total = total + lax.dot_general(
                wide_refs[slot, lag * GROUP : lag * GROUP + rows, :],
                taps,
                (((1,), (1,)), ((), ())),
                preferred_element_type=jnp.float32,
            )
        done = total.astype(jnp.bfloat16)
        first = group * GROUP
        for part in range(parts):
            row = (part // 2) * GROUP
            lane = (part % 2) * LANES
            out_ref[part, first : first + GROUP, :] = done[row : row + GROUP, lane : lane + LANES]

    prepare(0)
    for group in range(groups):
        if group + 1 < groups:
            prepare(group + 1)
        multiply(group)


def filter_kernel(blocks_ref, out_ref, tall_refs, saved_ref, product_refs):
    parts = blocks_ref.shape[0]
    rows = parts * GROUP
    groups = SIDE
    channels = groups * GROUP
    row_ids = lax.broadcasted_iota(jnp.int32, (LANES, LANES), 0)
    col_ids = lax.broadcasted_iota(jnp.int32, (LANES, LANES), 1)
    flip = jnp.where(row_ids + col_ids == LANES - 1, 1.0, 0.0).astype(jnp.bfloat16)
    empty = jnp.zeros((LANES, LANES), jnp.float32)
    for group in range(groups):
        product_refs[group, :, :LANES] = empty
        product_refs[group, :, (parts + 1) * LANES :] = empty
        tall_refs[group, rows - GROUP :, LANES:] = jnp.zeros((GROUP, LANES), jnp.bfloat16)

    def multiply(group):
        first = group * GROUP
        tall_ref, product_ref = tall_refs.at[group], product_refs.at[group]
        for part in range(parts):
            mine = blocks_ref[part, first : first + GROUP, :]
            here = slice(part * GROUP, (part + 1) * GROUP)
            tall_ref[here, :LANES] = mine
            if part > 0:
                tall_ref[(part - 1) * GROUP : part * GROUP, LANES:] = mine
            saved_ref[group, here, :] = blocks_ref[
                part, channels + first : channels + first + GROUP, :
            ]
        flipped = lax.dot_general(
            flip, saved_ref[group], (((1,), (1,)), ((), ())), preferred_element_type=jnp.float32
        ).astype(jnp.bfloat16)
        for pair in range(parts // 2):
            start = 2 * pair * GROUP
            depth = rows - start
            product_ref[:, LANES + pair * SPAN : LANES + (pair + 1) * SPAN] = jnp.dot(
                flipped[:, :depth], tall_ref[start:, :], preferred_element_type=jnp.float32
            )

    def add_up(group):
        turned = pltpu.roll(product_refs[group], 1, 1, stride=1, stride_axis=0)
        line = jnp.sum(turned, axis=0, keepdims=True)
        for part in range(parts):
            start = SPAN + part * LANES
            out_ref[group * parts + part] = line[:, start : start + LANES]

    for group in range(groups):
        multiply(group)
        if group > 0:
            add_up(group - 1)
    add_up(groups - 1)


def split_kernel(came_ref, keep_ref, send_ref, total_ref):
    parts = came_ref.shape[0] // SIDE
    places = parts // SIDE
    total = came_ref[:parts]
    for step in range(1, SIDE):
        total = total + came_ref[step * parts : (step + 1) * parts]
    total_ref[...] = total.reshape(parts, LANES)
    half = lax.axis_index("zh") // 2
    for low in range(2):
        here = slice(low * places, (low + 1) * places)
        mine, other = 2 * half + low, 2 * (1 - half) + low
        keep_ref[here, :] = total_ref[pl.ds(mine, places, stride=SIDE), :]
        send_ref[here, :] = total_ref[pl.ds(other, places, stride=SIDE), :]


def halve_kernel(kept_ref, came_ref, keep_ref, send_ref, total_ref):
    places = keep_ref.shape[0]
    total_ref[...] = kept_ref[...] + came_ref[...]
    half = lax.axis_index("zh") % 2
    keep_ref[...] = total_ref[pl.ds(pl.multiple_of(half * places, places), places), :]
    send_ref[...] = total_ref[pl.ds(pl.multiple_of((1 - half) * places, places), places), :]


def last_kernel(scale, blocks_ref, kept_ref, came_ref, input_ref, filter_ref):
    filter_ref[...] = (kept_ref[...] + came_ref[...]) * scale
    places = LANES // GROUP
    for tile in range(input_ref.shape[1] // LANES):
        slot, inner = tile // SIDE, tile % SIDE
        row = slot * GROUP
        rows = [
            blocks_ref[place * SIDE + inner, row : row + GROUP, :] for place in range(places)
        ]
        input_ref[:, tile * LANES : (tile + 1) * LANES] = jnp.concatenate(rows, axis=0).T


def on_device(u_saved, grad_out, filters):
    tokens, width = u_saved.shape[1:]
    parts = lax.axis_size(("y", "w"))
    seqs = lax.axis_size(("x", "zh"))
    places = lax.axis_size("y")
    channels = width // parts
    groups = channels // GROUP
    length = parts * LANES
    bf16, f32 = jnp.bfloat16, jnp.float32
    half_rows = parts // 2 * GROUP

    rows = 2 * channels + 8
    packed = call(
        pack_kernel,
        jax.ShapeDtypeStruct((places, SIDE, rows, LANES), bf16),
        *(
            pltpu.with_memory_space_constraint(array, pltpu.HBM)
            for array in (u_saved[0], grad_out[0], filters)
        ),
        scratch=[
            pltpu.VMEM((tokens, width), bf16),
            pltpu.VMEM((tokens, width), bf16),
            pltpu.VMEM(filters.shape, bf16),
            pltpu.VMEM((LANES, LANES), f32),
            pltpu.SemaphoreType.DMA((3,)),
        ],
        vmem=8 * MIB,
        space=pltpu.HBM,
    ).reshape(parts, rows, LANES)
    blocks = lax.all_to_all(packed, ("y", "w"), split_axis=0, concat_axis=0, tiled=True)
    lags = call(
        filter_kernel,
        jax.ShapeDtypeStruct((SIDE * parts, 1, LANES), f32),
        blocks,
        scratch=[
            pltpu.VMEM((groups, 2 * half_rows, SPAN), bf16),
            pltpu.VMEM((groups, 2 * half_rows, LANES), bf16),
            pltpu.VMEM((groups, LANES, length + SPAN), f32),
        ],
        flops=2**31,
        vmem=24 * MIB,
    )
    lags_came = lax.all_to_all(lags, ("x", "y", "w"), split_axis=0, concat_axis=0, tiled=True)
    input_blocks = call(
        input_kernel,
        jax.ShapeDtypeStruct((parts, channels, LANES), bf16),
        blocks,
        scratch=[
            pltpu.VMEM((groups, length + SPAN), f32),
            pltpu.VMEM((2, 2 * half_rows, SPAN), bf16),
            pltpu.VMEM((2, LANES, length + SPAN), bf16),
        ],
        flops=2**31,
        vmem=20 * MIB,
    )
    input_blocks, lags_came = lax.optimization_barrier((input_blocks, lags_came))
    returned = lax.all_to_all(input_blocks, ("y", "w"), split_axis=0, concat_axis=0, tiled=True)
    halves = [jax.ShapeDtypeStruct((2 * places, LANES), f32)] * 2
    whole_places = jax.ShapeDtypeStruct((places, LANES), f32)
    kept, sent = call(split_kernel, halves, lags_came, scratch=[pltpu.VMEM((parts, LANES), f32)])
    far = lax.ppermute(sent, "zh", [(side, side ^ 2) for side in range(SIDE)])
    kept, sent = call(
        halve_kernel,
        [whole_places] * 2,
        kept,
        far,
        scratch=[pltpu.VMEM((2 * places, LANES), f32)],
    )
    near = lax.ppermute(sent, "zh", [(side, side ^ 1) for side in range(SIDE)])
    scale = 1.0 / math.sqrt(GROUP * seqs * length)
    input_grad, filter_part = call(
        lambda *refs: last_kernel(scale, *refs),
        [jax.ShapeDtypeStruct((tokens, width), bf16), whole_places],
        returned,
        kept,
        near,
        vmem=4 * MIB,
    )
    return (input_grad[None], filter_part.T)


def solution(mesh):
    cut = Mesh(mesh.devices.reshape(SIDE, SIDE, -1, SIDE), ("x", "zh", "y", "w"))
    seq, token = ("x", "zh"), ("y", "w")
    in_specs = (P(seq, token, None), P(seq, token, None), P(token, None))
    out_specs = (P(seq, token, None), P(token, seq))
    return jax.shard_map(
        on_device, mesh=cut, in_specs=in_specs, out_specs=out_specs, check_vma=False
    )
```
